512 devices in a mesh: seq: 128 (over y, z_lo, x), chan: 4 (over z_hi, core).
Axes of the slice: x: 4, y: 8, z: 8 (z_hi: 2, z_lo: 4; z = z_hi * 4 + z_lo), core: 2. Of those that a mesh axis runs over, the one named last changes fastest.
Arguments:
- gate_in: bfloat16 [128, 16384], P('chan', 'seq'), may hold values from -6 to 6
- value_in: bfloat16 [128, 16384], P('chan', 'seq'), may hold values from -6 to 6
- out_gate: bfloat16 [128, 16384], P('chan', 'seq'), may hold values from -6 to 6
- filter_taps: bfloat16 [128, 16384], P('chan', 'seq'), may hold values from -0.046875 to 0.046875
- out_weight: bfloat16 [128, 8192], P(None, 'chan'), may hold values from -0.0625 to 0.0625
- out_grad: bfloat16 [16384, 8192], P('seq', 'chan'), may hold values from -6 to 6
Outputs:
- grad_gate: bfloat16 [128, 16384], P('chan', 'seq')
- grad_value: bfloat16 [128, 16384], P('chan', 'seq')
- grad_outgate: bfloat16 [128, 16384], P('chan', 'seq')
- grad_taps: float32 [128, 16384], P('chan', 'seq')
The draws below stay inside these ranges and needn't reach their ends.
All inputs are finite; a program needn't handle non-finite values.
Results may differ from the reference program's by a relative error of at most 0.011.
Values sent between devices are 32-bit elements; how exact they have to be, the bound alone decides.
No kernel may reach another device: no remote copies, remote signals or barrier semaphores. Data moves between devices by JAX's collectives and lax.ppermute only.
A program may use at most 64 MiB of HBM per device.

```python
import math
import jax
import jax.numpy as jnp

D = 8192
CH = 128
TOKENS = 16384


def levels(rng, dims, pieces, smallest, top_value):
    loudness = 1.0
    for dim, shards_of in pieces:
        draws = jax.random.uniform(jax.random.fold_in(jax.random.fold_in(rng, 6), dim), (shards_of,), jnp.float32, smallest / len(pieces), top_value / len(pieces))
        loudness = loudness * jnp.repeat(jnp.exp(draws), dims[dim] // shards_of).reshape((-1,) + (1,) * (len(dims) - 1 - dim))
    return loudness


def gaussian(key, extent, scale, reach, cuts=(), kind=jnp.bfloat16):
    entries = scale * jax.random.normal(key, extent, jnp.float32)
    if cuts:
        entries = entries * levels(key, extent, cuts, -0.22, 0.18)
    return jnp.clip(entries, -reach, reach).astype(kind)


def setup_inputs(seed: int = 0) -> dict:
    keys = jax.random.split(jax.random.key(seed), 7)
    gate_in = gaussian(keys[0], (CH, TOKENS), 1.0, 6.0, ((0, 4), (1, 128)))
    value_in = gaussian(keys[1], (CH, TOKENS), 1.0, 6.0, ((0, 4), (1, 128)))
    out_gate = gaussian(keys[2], (CH, TOKENS), 1.0, 6.0, ((0, 4), (1, 128)))
    filter_taps = gaussian(keys[3], (CH, TOKENS), TOKENS ** -0.5, 0.046875, ((0, 4), (1, 128)))
    out_weight = gaussian(keys[4], (CH, D), D ** -0.5, 0.0625, ((1, 4),))
    out_grad = gaussian(keys[5], (TOKENS, D), 1.0, 6.0, ((0, 128), (1, 4)))
    return {"gate_in": gate_in, "value_in": value_in, "out_gate": out_gate, "filter_taps": filter_taps, "out_weight": out_weight, "out_grad": out_grad}


def reference(gate_in, value_in, out_gate, filter_taps, out_weight, out_grad):
    gated_input = (gate_in.astype(jnp.float32) * value_in.astype(jnp.float32)).astype(jnp.bfloat16)
    length = 1 << (2 * TOKENS - 1).bit_length()
    gated_freq = jnp.fft.rfft(gated_input.astype(jnp.float32), n=length, axis=1)
    taps_freq = jnp.fft.rfft(filter_taps.astype(jnp.float32), n=length, axis=1)
    conv_out = jnp.fft.irfft(gated_freq * taps_freq, n=length, axis=1)[:, :TOKENS].astype(jnp.float32)
    grad_mix = jnp.dot(out_weight, out_grad.T, preferred_element_type=jnp.float32)
    grad_outgate = (grad_mix * conv_out).astype(jnp.bfloat16)
    grad_conv = (grad_mix * out_gate.astype(jnp.float32)).astype(jnp.bfloat16)
    grad_freq = jnp.fft.rfft(grad_conv.astype(jnp.float32), n=length, axis=1)
    grad_input = jnp.fft.irfft(grad_freq * jnp.conj(taps_freq), n=length, axis=1)[:, :TOKENS].astype(jnp.float32)
    grad_gate = (grad_input * value_in.astype(jnp.float32)).astype(jnp.bfloat16)
    grad_value = (grad_input * gate_in.astype(jnp.float32)).astype(jnp.bfloat16)
    taps_raw = jnp.fft.irfft(grad_freq * jnp.conj(gated_freq), n=length, axis=1)[:, :TOKENS].astype(jnp.float32)
    grad_taps = taps_raw * (1.0 / math.sqrt(TOKENS))
    return (grad_gate, grad_value, grad_outgate, grad_taps)
```

```python
import math

import jax
import jax.numpy as jnp
from jax import lax
from jax.experimental import pallas as pl
from jax.experimental.pallas import tpu as pltpu
from jax.sharding import Mesh
from jax.sharding import PartitionSpec as P

BLOCK = 128
SHARE = 32
GROUP = 8
SEQ = ("y_hi", "y_lo", "z", "x")
OWNERS = ("y_lo", "z", "x")
CHAN = ("z_hi", "core")


def correlate_kernel(start_ref, signal_ref, out_ref, gated_pad, grad_pad):
    start = start_ref[0]
    zeros = jnp.zeros((BLOCK, BLOCK), jnp.float32)
    grad_pad[:BLOCK, :] = signal_ref[:, :BLOCK]
    grad_pad[BLOCK:, :] = zeros
    gated_pad[:BLOCK, :] = zeros
    gated_pad[BLOCK:, :] = signal_ref[:, BLOCK : 2 * BLOCK]
    row = lax.broadcasted_iota(jnp.int32, (BLOCK, BLOCK), 0)
    col = lax.broadcasted_iota(jnp.int32, (BLOCK, BLOCK), 1)
    upper = col >= row

    def rolled(rows, index):
        wide = jnp.broadcast_to(rows[index : index + 1, :], (BLOCK, BLOCK))
        return pltpu.roll(wide, 0, 1, stride=1, stride_axis=0)

    def step(number, carry):
        last_taps, last_gated, conv, corr = carry
        base = pl.multiple_of(number * GROUP, GROUP)
        gated_rows = signal_ref[pl.ds(base, GROUP), BLOCK : 2 * BLOCK]
        taps_rows = signal_ref[pl.ds(base, GROUP), 2 * BLOCK :]
        taps_mats, gated_mats, gated_left, grad_left = [], [], [], []
        for index in range(GROUP):
            this_taps, this_gated = rolled(taps_rows, index), rolled(gated_rows, index)
            taps_mats.append(jnp.where(upper, this_taps, last_taps).astype(jnp.bfloat16))
            gated_mats.append(jnp.where(upper, this_gated, last_gated).astype(jnp.bfloat16))
            last_taps, last_gated = this_taps, this_gated
            block = base + index
            gated_left.append(gated_pad[pl.ds(BLOCK + start - block, SHARE), :])
            grad_left.append(grad_pad[pl.ds(start + block, SHARE), :])
        conv = conv + jnp.dot(
            jnp.concatenate(gated_left, 1).astype(jnp.bfloat16),
            jnp.concatenate(taps_mats, 0),
            preferred_element_type=jnp.float32,
        )
        corr = corr + lax.dot_general(
            jnp.concatenate(grad_left, 1).astype(jnp.bfloat16),
            jnp.concatenate(
                [jnp.concatenate(taps_mats, 1), jnp.concatenate(gated_mats, 1)], 0
            ),
            (((1,), (1,)), ((), ())),
            preferred_element_type=jnp.float32,
        )
        return last_taps, last_gated, conv, corr

    _, _, conv, corr = lax.fori_loop(
        0,
        BLOCK // GROUP,
        step,
        (
            zeros,
            zeros,
            jnp.zeros((SHARE, BLOCK), jnp.float32),
            jnp.zeros((SHARE, 2 * BLOCK), jnp.float32),
        ),
    )
    out_ref[:, :BLOCK] = conv
    out_ref[:, BLOCK:] = corr


def correlate(start, signals):
    return pl.pallas_call(
        correlate_kernel,
        out_shape=jax.ShapeDtypeStruct((SHARE, 3 * BLOCK), jnp.float32),
        in_specs=[
            pl.BlockSpec(memory_space=pltpu.SMEM),
            pl.BlockSpec(memory_space=pltpu.VMEM),
        ],
        out_specs=pl.BlockSpec(memory_space=pltpu.VMEM),
        scratch_shapes=[pltpu.VMEM((2 * BLOCK, BLOCK), jnp.float32)] * 2,
        compiler_params=pltpu.CompilerParams(vmem_limit_bytes=32 * 1024 * 1024),
        cost_estimate=pl.CostEstimate(
            flops=6 * SHARE * BLOCK**3, bytes_accessed=250000, transcendentals=0
        ),
        name="correlate",
    )(start, signals)


def local(gate_in, value_in, out_gate, filter_taps, out_weight, out_grad):
    channels, tok_rows = gate_in.shape
    gate, value = gate_in.astype(jnp.float32), value_in.astype(jnp.float32)
    gated = (gate * value).astype(jnp.bfloat16).astype(jnp.float32)
    taps = filter_taps.astype(jnp.float32)
    partial = lax.dot_general(
        out_weight, out_grad, (((1,), (1,)), ((), ())), preferred_element_type=jnp.float32
    ).reshape(2, 2, channels, tok_rows)
    core, half = lax.axis_index("core"), lax.axis_index("z_hi")
    swap = [(0, 1), (1, 0)]
    kept = jnp.where(core == 0, partial[:, 0], partial[:, 1])
    sent = jnp.where(core == 0, partial[:, 1], partial[:, 0])
    partial = kept + lax.ppermute(sent, "core", swap)
    kept = jnp.where(half == 0, partial[0], partial[1])
    sent = jnp.where(half == 0, partial[1], partial[0])
    grad_mix = kept + lax.ppermute(sent, "z_hi", swap)
    grad_conv = (grad_mix * out_gate.astype(jnp.float32)).astype(jnp.bfloat16)
    signals = jnp.concatenate([grad_conv.astype(jnp.float32), gated, taps], axis=1)
    signals = lax.all_to_all(
        jnp.concatenate([signals] * 4, axis=0), SEQ, split_axis=0, concat_axis=0, tiled=True
    )
    start = (lax.axis_index("y_hi") * SHARE).astype(jnp.int32).reshape(1)
    results = correlate(start, signals)
    results = lax.all_to_all(results, OWNERS, split_axis=0, concat_axis=0, tiled=True)
    conv, grad_input, grad_taps = (
        results[:, :BLOCK],
        results[:, BLOCK : 2 * BLOCK],
        results[:, 2 * BLOCK :],
    )
    grad_outgate = (grad_mix * conv).astype(jnp.bfloat16)
    grad_gate = (grad_input * value).astype(jnp.bfloat16)
    grad_value = (grad_input * gate).astype(jnp.bfloat16)
    return (grad_gate, grad_value, grad_outgate, grad_taps * (1.0 / math.sqrt(BLOCK * BLOCK)))


def solution(mesh):
    fine = Mesh(mesh.devices.reshape(4, 2, 4, 4, 2, 2), SEQ + CHAN)
    rows = P(CHAN, SEQ)
    return jax.shard_map(
        local,
        mesh=fine,
        in_specs=(rows, rows, rows, rows, P(None, CHAN), P(SEQ, CHAN)),
        out_specs=(rows, rows, rows, rows),
        check_vma=False,
    )
```

```python
import jax
import jax.numpy as jnp
import numpy as np
from jax import lax
from jax.experimental import pallas as pl
from jax.experimental.pallas import tpu as pltpu
from jax.sharding import Mesh
from jax.sharding import PartitionSpec as P

SIDE = 128
SHARE = 32
LENGTH = SIDE * SIDE
SEQ = ("y_hi", "y_lo", "z", "x")
OWNERS = ("y_lo", "z", "x")
CHAN = ("z_hi", "core")


def transform_tables():
    index = np.arange(SIDE)
    quarter = 4 * index + 1
    angle = 2 * np.pi * np.outer(quarter, index) / (4 * SIDE)
    rows = np.concatenate([np.cos(angle), -np.sin(angle)], axis=0)
    angle = 2 * np.pi * (np.outer(index, index) % SIDE) / SIDE
    cos, sin = np.cos(angle), np.sin(angle)
    columns = np.block([[cos, -sin], [sin, cos]])
    angle = 2 * np.pi * np.outer(quarter, index) / (4 * LENGTH)
    wave = np.concatenate([np.cos(angle), np.sin(angle)], axis=1)
    table = np.concatenate([columns, rows.T, wave], axis=0)
    return rows.astype(np.float32), table.astype(np.float32)


def product(left, right):
    return jnp.dot(left, right, preferred_element_type=jnp.float32)


def split(values):
    high = values.astype(jnp.bfloat16)
    return high, (values - high.astype(jnp.float32)).astype(jnp.bfloat16)


def wide_product(left, right):
    (left_high, left_low), (right_high, right_low) = left, right
    small = product(left_low, right_high) + product(left_high, right_low)
    return product(left_high, right_high) + small


def convolve_kernel(place_ref, signal_ref, rows_ref, table_ref, out_ref, mix_ref):
    n = SIDE
    own = pl.ds(pl.multiple_of(place_ref[0] * n, n), n)
    share = pl.multiple_of(place_ref[1] * SHARE, SHARE)
    grad_mix = signal_ref[:n, :n] + signal_ref[n:, :n]
    mix_ref[...] = grad_mix
    grad_conv = (grad_mix * signal_ref[own, 3 * n :]).astype(jnp.bfloat16)
    others = signal_ref[own, n : 3 * n].astype(jnp.bfloat16)
    signals = jnp.concatenate([grad_conv, others], axis=1)
    rows_high, rows_low = split(rows_ref[...])
    spread = product(rows_high, signals) + product(rows_low, signals)
    columns = split(table_ref[: 2 * n, :])
    cos, sin = table_ref[3 * n :, :n], table_ref[3 * n :, n:]
    turned = []
    for at in range(3):
        re, im = spread[:n, at * n : (at + 1) * n], spread[n:, at * n : (at + 1) * n]
        turned.append(jnp.concatenate([re * cos + im * sin, im * cos - re * sin], axis=1))
    spectra = wide_product(split(jnp.concatenate(turned, axis=0)), columns)
    grad_re, grad_im = spectra[:n, :n], spectra[:n, n:]
    gated_re, gated_im = spectra[n : 2 * n, :n], spectra[n : 2 * n, n:]
    taps_re, taps_im = spectra[2 * n :, :n], spectra[2 * n :, n:]
    pairs = [
        (gated_re * taps_re - gated_im * taps_im, -(gated_re * taps_im + gated_im * taps_re)),
        (grad_re * taps_re + grad_im * taps_im, grad_re * taps_im - grad_im * taps_re),
        (grad_re * gated_re + grad_im * gated_im, grad_re * gated_im - grad_im * gated_re),
    ]
    pairs = jnp.concatenate([jnp.concatenate(pair, axis=1) for pair in pairs], axis=0)
    back = wide_product(split(pairs), columns)
    turned = []
    for at in range(3):
        re, im = back[at * n : (at + 1) * n, :n], back[at * n : (at + 1) * n, n:]
        turned.append(jnp.concatenate([re * cos + im * sin, re * sin - im * cos], axis=0))
    last = split(table_ref[pl.ds(2 * n + share, SHARE), :])
    results = wide_product(last, split(jnp.concatenate(turned, axis=1))) * (1.0 / LENGTH)
    out_ref[:, :n] = results[:, :n] * mix_ref[pl.ds(share, SHARE), :]
    out_ref[:, n:] = results[:, n:]


def convolve(place, signals):
    rows, table = transform_tables()
    return pl.pallas_call(
        convolve_kernel,
        out_shape=jax.ShapeDtypeStruct((SHARE, 3 * SIDE), jnp.float32),
        in_specs=[pl.BlockSpec(memory_space=pltpu.SMEM)]
        + [pl.BlockSpec(memory_space=pltpu.VMEM)] * 3,
        out_specs=pl.BlockSpec(memory_space=pltpu.VMEM),
        scratch_shapes=[pltpu.VMEM((SIDE, SIDE), jnp.float32)],
        compiler_params=pltpu.CompilerParams(vmem_limit_bytes=32 * 1024 * 1024),
        cost_estimate=pl.CostEstimate(
            flops=400_000_000, bytes_accessed=1_200_000, transcendentals=0
        ),
        name="convolve",
    )(place, signals, jnp.asarray(rows), jnp.asarray(table))


def local(gate_in, value_in, out_gate, filter_taps, out_weight, out_grad):
    channels, tok_rows = gate_in.shape
    gate, value = gate_in.astype(jnp.float32), value_in.astype(jnp.float32)
    gated = (gate * value).astype(jnp.bfloat16).astype(jnp.float32)
    taps, outer = filter_taps.astype(jnp.float32), out_gate.astype(jnp.float32)
    partial = lax.dot_general(
        out_weight, out_grad, (((1,), (1,)), ((), ())), preferred_element_type=jnp.float32
    ).reshape(2, 2, channels, tok_rows)
    core, half = lax.axis_index("core"), lax.axis_index("z_hi")
    kept = jnp.where(core == 0, partial[:, 0], partial[:, 1])
    sent = jnp.where(core == 0, partial[:, 1], partial[:, 0])
    partial = kept + lax.ppermute(sent, "core", [(0, 1), (1, 0)])
    own = [gated, taps, outer]
    signals = [jnp.concatenate([partial[to], *own], axis=1) for to in range(2) for _ in range(4)]
    signals = lax.all_to_all(
        jnp.concatenate(signals, axis=0), ("z_hi",) + SEQ, split_axis=0, concat_axis=0, tiled=True
    )
    place = jnp.stack([half, lax.axis_index("y_hi")]).astype(jnp.int32)
    results = convolve(place, signals)
    results = lax.all_to_all(results, OWNERS, split_axis=0, concat_axis=0, tiled=True)
    grad_outgate, grad_input, grad_taps = (
        results[:, :SIDE],
        results[:, SIDE : 2 * SIDE],
        results[:, 2 * SIDE :],
    )
    grad_gate = (grad_input * value).astype(jnp.bfloat16)
    grad_value = (grad_input * gate).astype(jnp.bfloat16)
    return (grad_gate, grad_value, grad_outgate.astype(jnp.bfloat16), grad_taps * LENGTH**-0.5)


def solution(mesh):
    fine = Mesh(mesh.devices.reshape(4, 2, 4, 4, 2, 2), SEQ + CHAN)
    rows = P(CHAN, SEQ)
    return jax.shard_map(
        local,
        mesh=fine,
        in_specs=(rows, rows, rows, rows, P(None, CHAN), P(SEQ, CHAN)),
        out_specs=(rows, rows, rows, rows),
        check_vma=False,
    )
```

```python
import jax
import jax.numpy as jnp
import numpy as np
from jax import lax
from jax.experimental import pallas as pl
from jax.experimental.pallas import tpu as pltpu
from jax.sharding import Mesh
from jax.sharding import PartitionSpec as P

SIDE = 128
SHARE = 32
LENGTH = SIDE * SIDE
SEQ = ("y_hi", "y_lo", "z", "x")
OWNERS = ("y_lo", "z", "x")
CHAN = ("z_hi", "core")


def transform_tables():
    index = np.arange(SIDE)
    quarter = 4 * index + 1
    angle = 2 * np.pi * np.outer(quarter, index) / (4 * SIDE)
    rows = np.concatenate([np.cos(angle), -np.sin(angle)], axis=0)
    angle = 2 * np.pi * (np.outer(index, index) % SIDE) / SIDE
    cos, sin = np.cos(angle), np.sin(angle)
    columns = np.block([[cos, -sin], [sin, cos]])
    angle = 2 * np.pi * np.outer(quarter, index) / (4 * LENGTH)
    wave = np.concatenate([np.cos(angle), np.sin(angle)], axis=1)
    table = np.concatenate([columns, rows.T, wave], axis=0)
    return rows.astype(np.float32), table.astype(np.float32)


def product(left, right):
    return jnp.dot(left, right, preferred_element_type=jnp.float32)


def split(values):
    high = values.astype(jnp.bfloat16)
    return high, (values - high.astype(jnp.float32)).astype(jnp.bfloat16)


def wide_product(left, right):
    (left_high, left_low), (right_high, right_low) = left, right
    small = product(left_low, right_high) + product(left_high, right_low)
    return product(left_high, right_high) + small


def convolve_kernel(place_ref, signal_ref, rows_ref, table_ref, out_ref):
    n = SIDE
    share = pl.multiple_of(place_ref[0] * SHARE, SHARE)
    signals = signal_ref[...].astype(jnp.bfloat16)
    rows_high, rows_low = split(rows_ref[...])
    spread = product(rows_high, signals) + product(rows_low, signals)
    columns = split(table_ref[: 2 * n, :])
    cos, sin = table_ref[3 * n :, :n], table_ref[3 * n :, n:]
    turned = []
    for at in range(3):
        re, im = spread[:n, at * n : (at + 1) * n], spread[n:, at * n : (at + 1) * n]
        turned.append(jnp.concatenate([re * cos + im * sin, im * cos - re * sin], axis=1))
    spectra = wide_product(split(jnp.concatenate(turned, axis=0)), columns)
    grad_re, grad_im = spectra[:n, :n], spectra[:n, n:]
    gated_re, gated_im = spectra[n : 2 * n, :n], spectra[n : 2 * n, n:]
    taps_re, taps_im = spectra[2 * n :, :n], spectra[2 * n :, n:]
    pairs = [
        (gated_re * taps_re - gated_im * taps_im, -(gated_re * taps_im + gated_im * taps_re)),
        (grad_re * taps_re + grad_im * taps_im, grad_re * taps_im - grad_im * taps_re),
        (grad_re * gated_re + grad_im * gated_im, grad_re * gated_im - grad_im * gated_re),
    ]
    pairs = jnp.concatenate([jnp.concatenate(pair, axis=1) for pair in pairs], axis=0)
    back = wide_product(split(pairs), columns)
    turned = []
    for at in range(3):
        re, im = back[at * n : (at + 1) * n, :n], back[at * n : (at + 1) * n, n:]
        turned.append(jnp.concatenate([re * cos + im * sin, re * sin - im * cos], axis=0))
    last = split(table_ref[pl.ds(2 * n + share, SHARE), :])
    results = wide_product(last, split(jnp.concatenate(turned, axis=1))) * (1.0 / LENGTH)
    out_ref[...] = results


def convolve(place, signals):
    rows, table = transform_tables()
    return pl.pallas_call(
        convolve_kernel,
        out_shape=jax.ShapeDtypeStruct((SHARE, 3 * SIDE), jnp.float32),
        in_specs=[pl.BlockSpec(memory_space=pltpu.SMEM)]
        + [pl.BlockSpec(memory_space=pltpu.VMEM)] * 3,
        out_specs=pl.BlockSpec(memory_space=pltpu.VMEM),
        compiler_params=pltpu.CompilerParams(vmem_limit_bytes=32 * 1024 * 1024),
        cost_estimate=pl.CostEstimate(
            flops=400_000_000, bytes_accessed=1_200_000, transcendentals=0
        ),
        name="convolve",
    )(place, signals, jnp.asarray(rows), jnp.asarray(table))


def local(gate_in, value_in, out_gate, filter_taps, out_weight, out_grad):
    channels, tok_rows = gate_in.shape
    gate, value = gate_in.astype(jnp.float32), value_in.astype(jnp.float32)
    gated = (gate * value).astype(jnp.bfloat16).astype(jnp.float32)
    taps, outer = filter_taps.astype(jnp.float32), out_gate.astype(jnp.float32)
    partial = lax.dot_general(
        out_weight, out_grad, (((1,), (1,)), ((), ())), preferred_element_type=jnp.float32
    ).reshape(2, 2, channels, tok_rows)
    core, half = lax.axis_index("core"), lax.axis_index("z_hi")
    kept = jnp.where(core == 0, partial[:, 0], partial[:, 1])
    sent = jnp.where(core == 0, partial[:, 1], partial[:, 0])
    partial = kept + lax.ppermute(sent, "core", [(0, 1), (1, 0)])
    kept = jnp.where(half == 0, partial[0], partial[1])
    sent = jnp.where(half == 0, partial[1], partial[0])
    grad_mix = kept + lax.ppermute(sent, "z_hi", [(0, 1), (1, 0)])
    grad_conv = (grad_mix * outer).astype(jnp.bfloat16).astype(jnp.float32)
    signals = jnp.concatenate([grad_conv, gated, taps], axis=1)
    signals = lax.all_to_all(
        jnp.concatenate([signals] * 4, axis=0), SEQ, split_axis=0, concat_axis=0, tiled=True
    )
    place = lax.axis_index("y_hi").astype(jnp.int32).reshape(1)
    results = convolve(place, signals)
    results = lax.all_to_all(results, OWNERS, split_axis=0, concat_axis=0, tiled=True)
    conv, grad_input, grad_taps = (
        results[:, :SIDE],
        results[:, SIDE : 2 * SIDE],
        results[:, 2 * SIDE :],
    )
    grad_gate = (grad_input * value).astype(jnp.bfloat16)
    grad_value = (grad_input * gate).astype(jnp.bfloat16)
    return (grad_gate, grad_value, (grad_mix * conv).astype(jnp.bfloat16), grad_taps * LENGTH**-0.5)


def solution(mesh):
    fine = Mesh(mesh.devices.reshape(4, 2, 4, 4, 2, 2), SEQ + CHAN)
    rows = P(CHAN, SEQ)
    return jax.shard_map(
        local,
        mesh=fine,
        in_specs=(rows, rows, rows, rows, P(None, CHAN), P(SEQ, CHAN)),
        out_specs=(rows, rows, rows, rows),
        check_vma=False,
    )
```

```python
import jax
import jax.numpy as jnp
import numpy as np
from jax import lax
from jax.experimental import pallas as pl
from jax.experimental.pallas import tpu as pltpu
from jax.sharding import Mesh
from jax.sharding import PartitionSpec as P

SIDE = 128
SHARE = 32
LENGTH = SIDE * SIDE
CHUNKS = 2
SEQ = ("y_hi", "y_lo", "z", "x")
OWNERS = ("y_lo", "z", "x")
CHAN = ("z_hi", "core")


def transform_tables():
    index = np.arange(SIDE)
    quarter = 4 * index + 1
    angle = 2 * np.pi * np.outer(quarter, index) / (4 * SIDE)
    rows = np.concatenate([np.cos(angle), -np.sin(angle)], axis=0)
    angle = 2 * np.pi * (np.outer(index, index) % SIDE) / SIDE
    cos, sin = np.cos(angle), np.sin(angle)
    columns = np.block([[cos, -sin], [sin, cos]])
    angle = 2 * np.pi * np.outer(quarter, index) / (4 * LENGTH)
    wave = np.concatenate([np.cos(angle), np.sin(angle)], axis=1)
    table = np.concatenate([columns, rows.T, wave], axis=0)
    return rows.astype(np.float32), table.astype(np.float32)


def product(left, right):
    return jnp.dot(left, right, preferred_element_type=jnp.float32)


def split(values):
    high = values.astype(jnp.bfloat16)
    return high, (values - high.astype(jnp.float32)).astype(jnp.bfloat16)


def wide_product(left, right):
    (left_high, left_low), (right_high, right_low) = left, right
    small = product(left_low, right_high) + product(left_high, right_low)
    return product(left_high, right_high) + small


def convolve_kernel(place_ref, signal_ref, rows_ref, table_ref, out_ref):
    n = SIDE
    share = pl.multiple_of(place_ref[0] * SHARE, SHARE)
    signals = signal_ref[...].astype(jnp.bfloat16)
    rows_high, rows_low = split(rows_ref[...])
    spread = product(rows_high, signals) + product(rows_low, signals)
    columns = split(table_ref[: 2 * n, :])
    cos, sin = table_ref[3 * n :, :n], table_ref[3 * n :, n:]
    turned = []
    for at in range(3):
        re, im = spread[:n, at * n : (at + 1) * n], spread[n:, at * n : (at + 1) * n]
        turned.append(jnp.concatenate([re * cos + im * sin, im * cos - re * sin], axis=1))
    spectra = wide_product(split(jnp.concatenate(turned, axis=0)), columns)
    grad_re, grad_im = spectra[:n, :n], spectra[:n, n:]
    gated_re, gated_im = spectra[n : 2 * n, :n], spectra[n : 2 * n, n:]
    taps_re, taps_im = spectra[2 * n :, :n], spectra[2 * n :, n:]
    pairs = [
        (gated_re * taps_re - gated_im * taps_im, -(gated_re * taps_im + gated_im * taps_re)),
        (grad_re * taps_re + grad_im * taps_im, grad_re * taps_im - grad_im * taps_re),
        (grad_re * gated_re + grad_im * gated_im, grad_re * gated_im - grad_im * gated_re),
    ]
    pairs = jnp.concatenate([jnp.concatenate(pair, axis=1) for pair in pairs], axis=0)
    back = wide_product(split(pairs), columns)
    turned = []
    for at in range(3):
        re, im = back[at * n : (at + 1) * n, :n], back[at * n : (at + 1) * n, n:]
        turned.append(jnp.concatenate([re * cos + im * sin, re * sin - im * cos], axis=0))
    last = split(table_ref[pl.ds(2 * n + share, SHARE), :])
    results = wide_product(last, split(jnp.concatenate(turned, axis=1))) * (1.0 / LENGTH)
    out_ref[...] = results


def convolve(place, signals):
    rows, table = transform_tables()
    return pl.pallas_call(
        convolve_kernel,
        out_shape=jax.ShapeDtypeStruct((SHARE, 3 * SIDE), jnp.float32),
        in_specs=[pl.BlockSpec(memory_space=pltpu.SMEM)]
        + [pl.BlockSpec(memory_space=pltpu.VMEM)] * 3,
        out_specs=pl.BlockSpec(memory_space=pltpu.VMEM),
        compiler_params=pltpu.CompilerParams(vmem_limit_bytes=32 * 1024 * 1024),
        cost_estimate=pl.CostEstimate(
            flops=400_000_000, bytes_accessed=1_200_000, transcendentals=0
        ),
        name="convolve",
    )(place, signals, jnp.asarray(rows), jnp.asarray(table))


def mix_kernel(weight_hbm, grad_hbm, kept_ref, sent_ref, weight, grad, total, sems):
    copies = []
    for at in range(CHUNKS):
        columns = pl.ds(at * (weight.shape[1] // CHUNKS), weight.shape[1] // CHUNKS)
        pair = []
        for number, (source, target) in enumerate(((weight_hbm, weight), (grad_hbm, grad))):
            copy = pltpu.make_async_copy(
                source.at[:, columns], target.at[:, columns], sems.at[number, at]
            )
            copy.start()
            pair.append(copy)
        copies.append((columns, pair))
    partial = jnp.zeros(total.shape, jnp.float32)
    for columns, pair in copies:
        for copy in pair:
            copy.wait()
        partial = partial + lax.dot_general(
            weight[:, columns],
            grad[:, columns],
            (((1,), (1,)), ((), ())),
            preferred_element_type=jnp.float32,
        )
    total[...] = partial
    channels = kept_ref.shape[1]
    core = lax.axis_index("core")
    for half in range(2):
        own = pl.multiple_of((2 * half + core) * channels, channels)
        other = pl.multiple_of((2 * half + 1 - core) * channels, channels)
        kept_ref[half] = total[pl.ds(own, channels), :]
        sent_ref[half] = total[pl.ds(other, channels), :]


def partial_mix(weight, grad, channels):
    return pl.pallas_call(
        mix_kernel,
        out_shape=[jax.ShapeDtypeStruct((2, channels, SIDE), jnp.float32)] * 2,
        in_specs=[pl.BlockSpec(memory_space=pltpu.HBM)] * 2,
        out_specs=[pl.BlockSpec(memory_space=pltpu.VMEM)] * 2,
        scratch_shapes=[
            pltpu.VMEM(weight.shape, weight.dtype),
            pltpu.VMEM(grad.shape, grad.dtype),
            pltpu.VMEM((4 * channels, SIDE), jnp.float32),
            pltpu.SemaphoreType.DMA((2, CHUNKS)),
        ],
        compiler_params=pltpu.CompilerParams(vmem_limit_bytes=int(53.6 * 1024 * 1024)),
        name="partial_mix",
    )(weight, grad)


def local(gate_in, value_in, out_gate, filter_taps, out_weight, out_grad):
    channels = gate_in.shape[0]
    gate, value = gate_in.astype(jnp.float32), value_in.astype(jnp.float32)
    gated = (gate * value).astype(jnp.bfloat16).astype(jnp.float32)
    taps, outer = filter_taps.astype(jnp.float32), out_gate.astype(jnp.float32)
    half = lax.axis_index("z_hi")
    kept, sent = partial_mix(out_weight, out_grad, channels)
    partial = kept + lax.ppermute(sent, "core", [(0, 1), (1, 0)])
    kept = jnp.where(half == 0, partial[0], partial[1])
    sent = jnp.where(half == 0, partial[1], partial[0])
    grad_mix = kept + lax.ppermute(sent, "z_hi", [(0, 1), (1, 0)])
    grad_conv = (grad_mix * outer).astype(jnp.bfloat16).astype(jnp.float32)
    signals = jnp.concatenate([grad_conv, gated, taps], axis=1)
    signals = lax.all_to_all(
        jnp.concatenate([signals] * 4, axis=0), SEQ, split_axis=0, concat_axis=0, tiled=True
    )
    place = lax.axis_index("y_hi").astype(jnp.int32).reshape(1)
    results = convolve(place, signals)
    results = lax.all_to_all(results, OWNERS, split_axis=0, concat_axis=0, tiled=True)
    conv, grad_input, grad_taps = (
        results[:, :SIDE],
        results[:, SIDE : 2 * SIDE],
        results[:, 2 * SIDE :],
    )
    grad_gate = (grad_input * value).astype(jnp.bfloat16)
    grad_value = (grad_input * gate).astype(jnp.bfloat16)
    return (grad_gate, grad_value, (grad_mix * conv).astype(jnp.bfloat16), grad_taps * LENGTH**-0.5)


def solution(mesh):
    fine = Mesh(mesh.devices.reshape(4, 2, 4, 4, 2, 2), SEQ + CHAN)
    rows = P(CHAN, SEQ)
    return jax.shard_map(
        local,
        mesh=fine,
        in_specs=(rows, rows, rows, rows, P(None, CHAN), P(SEQ, CHAN)),
        out_specs=(rows, rows, rows, rows),
        check_vma=False,
    )
```
